512 devices in a mesh: grp: 16 (over z_hi, y, core), inp: 32 (over z_lo, x).
Axes of the slice: x: 4, y: 4, z: 16 (z_hi: 2, z_lo: 8; z = z_hi * 8 + z_lo), core: 2. Of those that a mesh axis runs over, the one named last changes fastest.
Arguments:
- samples: bfloat16 [512, 2097152], P('inp', 'grp'), may hold values from -6 to 6
- channel_index: int32 [128], replicated, may hold values from 0 to 1023, as said below
- tile_order: int32 [10, 2], replicated, may hold values from 0 to 3, as said below
Outputs:
- visibility: float32 [128, 10, 2, 128, 128], P('inp', None, None, 'grp')
The draws below stay inside these ranges and needn't reach their ends.
Inputs may be any that keep to these rules, and one draw needn't show every extreme that they name: `channel_index`: 128 distinct channel numbers. `tile_order`: each pair (r, q) of tiles with r >= q, of the 4 tiles of streams, appears exactly once.
All inputs are finite; a program needn't handle non-finite values.
Results may differ from the reference program's by a relative error of at most 0.013.
Values may be sent and summed in bfloat16 or wider, within the bound.
A program may use at most 64 MiB of HBM per device.

```python
import math
import jax
import jax.numpy as jnp
import numpy as np
from jax import lax

FFT = 2048
NCH = 1024
TAPS = 16
SEL = 128
STREAMS = 512
TILE = 128
FRAMES = 64
SAMPLES = 2097152
N_GRP = 16


def draw_channel_index(key, part):
    key = jax.random.fold_in(key, 11)
    return jax.random.permutation(key, NCH)[:SEL].astype(jnp.int32)


def draw_tile_order(key, part):
    key = jax.random.fold_in(key, 23)
    tile_count = STREAMS // TILE
    pair_table = np.array([[row_tile, col_tile] for row_tile in range(tile_count) for col_tile in range(row_tile + 1)], dtype=np.int32)
    shuffled = jax.random.permutation(key, pair_table.shape[0])
    return jnp.asarray(pair_table)[shuffled].astype(jnp.int32)


def level_of(key, shape, cuts, smallest, top_value):
    def one(axis_at, shards_of):
        heights = jax.random.uniform(jax.random.fold_in(jax.random.fold_in(key, 6), axis_at), (shards_of,), jnp.float32, smallest / len(cuts), top_value / len(cuts))
        return jnp.repeat(jnp.exp(heights), shape[axis_at] // shards_of).reshape((-1,) + (1,) * (len(shape) - axis_at - 1))

    factor_of = one(*cuts[0])
    for cut in cuts[1:]:
        factor_of = factor_of * one(*cut)
    return factor_of


def gaussian(key, dims, deviation, bound, shards=(), kind=jnp.bfloat16):
    entries = deviation * jax.random.normal(key, dims, jnp.float32)
    if shards:
        entries = entries * level_of(key, dims, shards, -0.22, 0.18)
    return jnp.clip(entries, -bound, bound).astype(kind)


def setup_inputs(seed: int = 0) -> dict:
    seeds = jax.random.split(jax.random.key(seed), 4)
    return {
        "samples": gaussian(seeds[0], (STREAMS, SAMPLES), 1.0, 6.0, ((0, 32), (1, 16))),
        "channel_index": draw_channel_index(jax.random.fold_in(seeds[3], 71), 0),
        "tile_order": draw_tile_order(jax.random.fold_in(seeds[3], 71), 0),
    }


def pfb_window():
    length = TAPS * FFT
    position = jnp.arange(length, dtype=jnp.int32).astype(jnp.float32)
    offset = (position - length // 2 + 0.5) / FFT
    sinc_part = jnp.sin(math.pi * offset) / (math.pi * offset)
    hamming = 0.54 - 0.46 * jnp.cos(2.0 * math.pi * position / (length - 1))
    shaped = (sinc_part * hamming).reshape(TAPS, FFT)
    power_mean = jnp.sum(shaped * shaped) / FFT
    return shaped / jnp.sqrt(power_mean)

def dft_table(channel_index):
    column = jnp.arange(FFT, dtype=jnp.int32)
    phase_index = channel_index.astype(jnp.int32)[:, None] * column[None, :] % FFT
    angles = 2.0 * math.pi / FFT * phase_index.astype(jnp.float32)
    scaling = 1.0 / math.sqrt(FFT)
    return jnp.stack([jnp.cos(angles) * scaling, -jnp.sin(angles) * scaling], axis=1).astype(jnp.bfloat16)

def reference(samples, channel_index, tile_order):
    window = pfb_window()
    table = dft_table(channel_index).astype(jnp.float32)
    spectra_count = FRAMES * N_GRP
    stream_group = min(16, STREAMS)
    history = (TAPS - 1) * FFT

    def channelize(stream_block):
        padded = jnp.concatenate([jnp.zeros((stream_group, history), jnp.float32), stream_block.astype(jnp.float32)], axis=1)
        frames = padded.reshape(stream_group, spectra_count + TAPS - 1, FFT)
        filtered = jnp.zeros((stream_group, spectra_count, FFT), jnp.float32)
        for tap_index in range(TAPS):
            filtered = filtered + window[tap_index] * frames[:, tap_index:tap_index + spectra_count]
        filtered = lax.optimization_barrier(filtered.astype(jnp.bfloat16)).astype(jnp.float32)
        spectra = jnp.einsum('ckp,sfp->cskf', table, filtered)
        return spectra.astype(jnp.bfloat16)
    stream_blocks = samples.reshape(STREAMS // stream_group, stream_group, SAMPLES)
    channelized = lax.map(channelize, stream_blocks)
    channelized = jnp.transpose(channelized, (1, 0, 2, 3, 4)).reshape(SEL, STREAMS, 2, spectra_count)
    scaling = 1.0 / math.sqrt(spectra_count)
    rows_index = tile_order[:, 0]
    cols_index = tile_order[:, 1]
    blocks_count = STREAMS // TILE

    def correlate(voltages):
        blocked = voltages.reshape(STREAMS, 2, N_GRP, FRAMES).transpose(2, 0, 1, 3)
        blocked = blocked.reshape(N_GRP, STREAMS, 2 * FRAMES).astype(jnp.float32)
        real_part = blocked[..., :FRAMES]
        imag_part = blocked[..., FRAMES:]
        turned = jnp.concatenate([imag_part, -real_part], axis=-1)
        stacked = jnp.stack([blocked, turned], axis=1)
        partial_value = jnp.einsum('gkaf,gbf->gkab', stacked, blocked) * scaling
        partial_value = lax.optimization_barrier(partial_value.astype(jnp.bfloat16)).astype(jnp.float32)
        summed = lax.optimization_barrier(jnp.sum(partial_value, axis=0))
        tile_grid = summed.reshape(2, blocks_count, TILE, blocks_count, TILE)
        return tile_grid[:, rows_index, :, cols_index, :]
    return lax.map(correlate, channelized)
```

```python
import math

import jax
import jax.numpy as jnp
import numpy as np
from jax import lax
from jax.experimental import pallas as pl
from jax.experimental.pallas import tpu as pltpu
from jax.sharding import PartitionSpec as P

FFT = 2048
TAPS = 16
TILE = 128
LANES = 128
MESH = pl.DeviceIdType.MESH
F32 = jnp.float32
BF16 = jnp.bfloat16
VMEM = pl.BlockSpec(memory_space=pltpu.VMEM)
LIMIT = 48 * 1024 * 1024


def pfb_window():
    length = TAPS * FFT
    position = np.arange(length, dtype=np.float64)
    offset = (position - length // 2 + 0.5) / FFT
    shaped = np.sinc(offset) * (0.54 - 0.46 * np.cos(2.0 * np.pi * position / (length - 1)))
    shaped = shaped / np.sqrt(np.sum(shaped * shaped) / FFT)
    return shaped.reshape(TAPS, FFT).astype(np.float32)


def nt_dot(a, b):
    return lax.dot_general(a, b, (((1,), (1,)), ((), ())), preferred_element_type=F32)


def wide(held, rows):
    return jnp.concatenate([held[a, rows].astype(BF16) for a in range(held.shape[0])], axis=1)


def fir(x_ref, taps, lane, first, count, frames):
    sums = [None] * count
    for frame in range(max(first - TAPS + 1, 0), min(first + count, frames)):
        value = x_ref[:, pl.ds(frame * FFT + lane, LANES)].astype(F32)
        for at in range(count):
            tap = frame - (first + at) + TAPS - 1
            if 0 <= tap < TAPS:
                term = taps[tap] * value
                sums[at] = term if sums[at] is None else sums[at] + term
    return sums


def load_taps(w_ref, lane):
    return [w_ref[pl.ds(k, 1), pl.ds(lane, LANES)] for k in range(TAPS)]


def table_and_tail_kernel(index_ref, x_ref, w_ref, table_ref, tail_ref, held):
    channels = index_ref.shape[1]
    streams = x_ref.shape[0]
    frames = x_ref.shape[1] // FFT
    step = 2.0 * math.pi / FFT
    channel = jnp.transpose(jnp.broadcast_to(index_ref[...], (channels, channels)))
    column = lax.broadcasted_iota(jnp.int32, (channels, channels), 1)
    fine = ((channel * column) % FFT).astype(F32) * step
    coarse = ((channel * (column * LANES)) % FFT).astype(F32) * step
    scale = 1.0 / math.sqrt(FFT)
    fine_cos, fine_sin = jnp.cos(fine) * scale, jnp.sin(fine) * scale
    coarse_cos, coarse_sin = jnp.cos(coarse), jnp.sin(coarse)
    for a in range(FFT // LANES):
        c, s = coarse_cos[:, a : a + 1], coarse_sin[:, a : a + 1]
        lanes = slice(a * LANES, (a + 1) * LANES)
        table_ref[0:channels, lanes] = (c * fine_cos - s * fine_sin).astype(BF16)
        table_ref[channels:, lanes] = (-(s * fine_cos + c * fine_sin)).astype(BF16)

    def chunk(at, carry):
        lane = pl.multiple_of(at * LANES, LANES)
        taps = load_taps(w_ref, lane)
        for first in (0, 8):
            sums = fir(x_ref, taps, lane, frames + first, 8, frames)
            for o, value in enumerate(sums):
                if value is None:
                    value = jnp.zeros((streams, LANES), F32)
                held[at, pl.ds(first + o, streams, stride=TAPS), :] = value
        return carry

    lax.fori_loop(0, FFT // LANES, chunk, 0)
    tail_ref[...] = nt_dot(table_ref[...], wide(held, slice(None))).astype(BF16)


def main_kernel(table_ref, x_ref, w_ref, out_ref, held):
    streams = x_ref.shape[0]
    frames = x_ref.shape[1] // FFT

    def chunk(at, carry):
        lane = pl.multiple_of(at * LANES, LANES)
        taps = load_taps(w_ref, lane)
        for first in range(0, frames, 8):
            sums = fir(x_ref, taps, lane, first, 8, frames)
            for o, value in enumerate(sums):
                held[at, pl.ds(first + o, streams, stride=frames), :] = value
        return carry

    lax.fori_loop(0, FFT // LANES, chunk, 0)
    for part in range(out_ref.shape[0]):
        rows = slice(part * 4 * frames, (part + 1) * 4 * frames)
        out_ref[part] = nt_dot(table_ref[...], wide(held, rows))


def exchange_kernel(
    d_ref, t_ref, out_ref, stage, send, v, p, r1, r2, keep, s3, r3, a_send, a_recv, c_send, c_recv, y_send, y_recv, z_send, z_recv
):
    channels, peers = v.shape[0], lax.axis_size("inp")
    me, g = lax.axis_index("inp"), lax.axis_index("grp")
    core, y, z = g % 2, (g // 2) % 4, g // 8
    rows = out_ref.shape[1]
    frames = LANES // 2

    barrier = pltpu.get_barrier_semaphore()

    def greet(d, carry):
        pl.semaphore_signal(barrier, inc=1, device_id={"inp": lax.rem(me + d, peers)}, device_id_type=MESH)
        return carry

    def y_peer(d):
        return z * 8 + ((y + d) % 4) * 2 + core

    core_peer = g + 1 - 2 * core
    z_peer = (1 - z) * 8 + y * 2 + core
    lax.fori_loop(1, peers, greet, 0)
    for other in (core_peer, y_peer(1), y_peer(2), y_peer(3), z_peer):
        pl.semaphore_signal(barrier, inc=1, device_id={"grp": other}, device_id_type=MESH)

    total = d_ref.shape[1] // 2
    source = lax.broadcasted_iota(jnp.int32, (256, 256), 0)
    target = lax.broadcasted_iota(jnp.int32, (256, 256), 1)
    low = lax.broadcasted_iota(jnp.int32, (total, LANES), 1) < frames
    for part in range(d_ref.shape[0]):
        same = (source // TAPS == target // frames + part * 4) & (source % TAPS == target % frames)
        spectra = d_ref[part] + jnp.dot(t_ref[...], same.astype(F32).astype(BF16), preferred_element_type=F32)
        for pair in range(2):
            re = spectra[0:total, pair * LANES : (pair + 1) * LANES]
            im = spectra[total:, pair * LANES : (pair + 1) * LANES]
            stream = part * 4 + pair * 2
            stage[pl.ds(stream, total, stride=16), :] = jnp.where(low, re, pltpu.roll(im, frames, 1))
            stage[pl.ds(stream + 1, total, stride=16), :] = jnp.where(low, pltpu.roll(re, frames, 1), im)
    send[...] = stage[...].astype(BF16)

    pl.semaphore_wait(barrier, peers - 1 + 5)

    def turn(c):
        def one(d, carry):
            j = lax.rem(me + d, peers)
            pltpu.make_async_remote_copy(
                src_ref=send.at[pl.ds(pl.multiple_of((j * channels + c) * 16, 16), 16)],
                dst_ref=v.at[c, pl.ds(pl.multiple_of(me * 16, 16), 16)],
                send_sem=a_send.at[c],
                recv_sem=a_recv.at[c],
                device_id={"inp": j},
                device_id_type=MESH,
            ).start()
            return carry

        lax.fori_loop(1, peers, one, 0)

    def turn_wait(c, sem):
        part = v.at[c, pl.ds(0, (peers - 1) * 16)]
        pltpu.make_async_copy(part, part, sem.at[c]).wait()

    def core_copy(c):
        return pltpu.make_async_remote_copy(
            src_ref=p.at[c, 1 - core],
            dst_ref=r1.at[c],
            send_sem=c_send.at[c],
            recv_sem=c_recv.at[c],
            device_id={"grp": core_peer},
            device_id_type=MESH,
        )

    def y_copy(c, d):
        return pltpu.make_async_remote_copy(
            src_ref=p.at[c, core, (y + d) % 4],
            dst_ref=r2.at[c, d - 1],
            send_sem=y_send.at[c, d - 1],
            recv_sem=y_recv.at[c, d - 1],
            device_id={"grp": y_peer(d)},
            device_id_type=MESH,
        )

    def z_copy(c):
        return pltpu.make_async_remote_copy(
            src_ref=s3.at[c],
            dst_ref=r3.at[c],
            send_sem=z_send.at[c],
            recv_sem=z_recv.at[c],
            device_id={"grp": z_peer},
            device_id_type=MESH,
        )

    for c in range(channels):
        turn(c)
    sign = jnp.where(lax.broadcasted_iota(jnp.int32, (TILE, LANES), 1) < frames, 1.0, -1.0) / 32.0
    tiles = v.shape[1] // TILE

    def products(c):
        for r in range(tiles):
            value = v[c, r * TILE : (r + 1) * TILE].astype(F32)
            turned = (pltpu.roll(value, frames, 1) * sign).reshape(16, 8, LANES)
            value = (value / 32.0).reshape(16, 8, LANES)
            order = [zz * 8 + yy * 2 + cc for cc in range(2) for yy in range(4) for zz in range(2)]
            left = jnp.concatenate([part for o in order for part in (value[o], turned[o])], axis=0).astype(BF16)
            for q in range(r + 1):
                t = r * (r + 1) // 2 + q
                got = nt_dot(left, v[c, q * TILE : (q + 1) * TILE]).astype(BF16)
                p[c, :, :, :, t * 16 : (t + 1) * 16, :] = got.reshape(2, 4, 2, 16, LANES)

    def core_sum(c):
        core_copy(c).wait_recv()
        for yy in range(4):
            p[c, core, yy] = (p[c, core, yy].astype(F32) + r1[c, yy].astype(F32)).astype(BF16)
        for d in range(1, 4):
            y_copy(c, d).start()

    def y_sum(c):
        for d in range(1, 4):
            y_copy(c, d).wait_recv()
        for zz in (z, 1 - z):
            got = p[c, core, y, zz].astype(F32)
            for d in range(3):
                got = got + r2[c, d, zz].astype(F32)
            if zz is z:
                keep[c] = got
            else:
                s3[c] = got.astype(BF16)
        z_copy(c).start()

    for c in range(channels):
        turn_wait(c, a_recv)
        own = pl.multiple_of((me * channels + c) * 16, 16)
        v[c, pl.ds(pl.multiple_of(me * 16, 16), 16)] = send[pl.ds(own, 16)]
        products(c)
        core_copy(c).start()
        if c:
            y_sum(c - 1)
        core_sum(c)
    y_sum(channels - 1)
    for c in range(channels):
        z_copy(c).wait_recv()
        out_ref[c] = keep[c] + r3[c].astype(F32)
    for c in range(channels):
        turn_wait(c, a_send)
        core_copy(c).wait_send()
        for d in range(1, 4):
            y_copy(c, d).wait_send()
        z_copy(c).wait_send()


def order_kernel(order_ref, in_ref, out_ref):
    for t in range(out_ref.shape[1]):
        r, q = order_ref[2 * t], order_ref[2 * t + 1]
        at = r * (r + 1) // 2 + q
        out_ref[:, pl.ds(t, 1)] = in_ref[:, pl.ds(at, 1)]


def table_and_tail(samples, channel_index, window):
    streams, selected = samples.shape[0], channel_index.shape[0]
    return pl.pallas_call(
        table_and_tail_kernel,
        out_shape=(
            jax.ShapeDtypeStruct((2 * selected, FFT), BF16),
            jax.ShapeDtypeStruct((2 * selected, streams * TAPS), BF16),
        ),
        in_specs=[VMEM] * 3,
        out_specs=(VMEM, VMEM),
        scratch_shapes=[pltpu.VMEM((FFT // LANES, streams * TAPS, LANES), F32)],
        compiler_params=pltpu.CompilerParams(vmem_limit_bytes=LIMIT),
        name="table_and_tail",
    )(channel_index.reshape(1, selected), samples, window)


def filter_and_dft(table, samples, window):
    streams, selected, frames = samples.shape[0], table.shape[0] // 2, samples.shape[1] // FFT
    return pl.pallas_call(
        main_kernel,
        out_shape=jax.ShapeDtypeStruct((streams // 4, 2 * selected, 4 * frames), F32),
        in_specs=[VMEM] * 3,
        out_specs=VMEM,
        scratch_shapes=[pltpu.VMEM((FFT // LANES, streams * frames, LANES), F32)],
        compiler_params=pltpu.CompilerParams(vmem_limit_bytes=LIMIT),
        cost_estimate=pl.CostEstimate(flops=2 * streams * frames * FFT * (TAPS + 2 * selected), bytes_accessed=8 << 20, transcendentals=0),
        name="filter_and_dft",
    )(table, samples, window)


def shards(samples, channel_index, tile_order):
    streams, length = samples.shape
    selected = channel_index.shape[0]
    peers = lax.axis_size("inp")
    group = lax.axis_size("grp")
    channels = selected // peers
    tile_count = tile_order.shape[0]
    window = jnp.asarray(pfb_window())

    table, tail = table_and_tail(samples, channel_index, window)
    earlier = lax.ppermute(tail, "grp", [(i, i + 1) for i in range(group - 1)])
    main = filter_and_dft(table, samples, window)
    dma = pltpu.SemaphoreType.DMA
    rows = tile_count * 16
    summed = pl.pallas_call(
        exchange_kernel,
        out_shape=jax.ShapeDtypeStruct((channels, rows, LANES), F32),
        in_specs=[VMEM] * 2,
        out_specs=VMEM,
        scratch_shapes=[
            pltpu.VMEM((selected * streams, LANES), F32),
            pltpu.VMEM((selected * streams, LANES), BF16),
            pltpu.VMEM((channels, peers * streams, LANES), BF16),
            pltpu.VMEM((channels, 2, 4, 2, rows, LANES), BF16),
            pltpu.VMEM((channels, 4, 2, rows, LANES), BF16),
            pltpu.VMEM((channels, 3, 2, rows, LANES), BF16),
            pltpu.VMEM((channels, rows, LANES), F32),
            pltpu.VMEM((channels, rows, LANES), BF16),
            pltpu.VMEM((channels, rows, LANES), BF16),
            dma((channels,)),
            dma((channels,)),
            dma((channels,)),
            dma((channels,)),
            dma((channels, 3)),
            dma((channels, 3)),
            dma((channels,)),
            dma((channels,)),
        ],
        compiler_params=pltpu.CompilerParams(collective_id=0, has_side_effects=True, vmem_limit_bytes=LIMIT),
        name="exchange",
    )(main, earlier)
    return pl.pallas_call(
        order_kernel,
        out_shape=jax.ShapeDtypeStruct((channels, tile_count, 2, 8, LANES), F32),
        in_specs=[pl.BlockSpec(memory_space=pltpu.SMEM), VMEM],
        out_specs=VMEM,
        name="tile_order",
    )(tile_order.reshape(-1), summed.reshape(channels, tile_count, 2, 8, LANES))


def solution(mesh):
    in_specs = (P("inp", "grp"), P(), P())
    out_specs = P("inp", None, None, "grp", None)
    return jax.shard_map(shards, mesh=mesh, in_specs=in_specs, out_specs=out_specs, check_vma=False)
```

```python
import math

import jax
import jax.numpy as jnp
import numpy as np
from jax import lax
from jax.experimental import pallas as pl
from jax.experimental.pallas import tpu as pltpu
from jax.sharding import PartitionSpec as P

FFT = 2048
TAPS = 16
TILE = 128
LANES = 128
CHUNKS = FFT // LANES
MESH = pl.DeviceIdType.MESH
F32 = jnp.float32
BF16 = jnp.bfloat16


def pfb_window():
    length = TAPS * FFT
    position = np.arange(length, dtype=np.float64)
    offset = (position - length // 2 + 0.5) / FFT
    shaped = np.sinc(offset) * (0.54 - 0.46 * np.cos(2.0 * np.pi * position / (length - 1)))
    shaped = shaped / np.sqrt(np.sum(shaped * shaped) / FFT)
    return shaped.reshape(TAPS, FFT).astype(np.float32)


def nt_dot(a, b):
    return lax.dot_general(a, b, (((1,), (1,)), ((), ())), preferred_element_type=F32)


def is_inner(tap):
    return TAPS // 2 - 2 <= tap < TAPS // 2 + 2


def fir(x_ref, w_ref, filt, at, first, count, row):
    streams, frames = x_ref.shape[0], x_ref.shape[1] // FFT
    lane = pl.multiple_of(at * LANES, LANES)
    taps = []
    for k in range(TAPS):
        weight = w_ref[pl.ds(k, 1), pl.ds(lane, LANES)]
        taps.append(weight if is_inner(k) else jnp.broadcast_to(weight, (streams, LANES)).astype(BF16))
    for start in range(first, first + count, 8):
        inner, outer = [None] * 8, [None] * 8
        for frame in range(max(start - TAPS + 1, 0), min(start + 8, frames)):
            value = x_ref[:, pl.ds(frame * FFT + lane, LANES)]
            wide = value.astype(F32)
            for o in range(8):
                tap = frame - (start + o) + TAPS - 1
                if not 0 <= tap < TAPS:
                    continue
                sums, term = (inner, taps[tap] * wide) if is_inner(tap) else (outer, taps[tap] * value)
                sums[o] = term if sums[o] is None else sums[o] + term
        for o in range(8):
            total = inner[o]
            if outer[o] is not None:
                total = outer[o].astype(F32) if total is None else total + outer[o].astype(F32)
            total = jnp.zeros((streams, LANES), F32) if total is None else total
            to = row + (start - first + o) * streams
            filt[to : to + streams, pl.ds(lane, LANES)] = total.astype(BF16)


def make_table(index_ref, picked, table):
    count = index_ref.shape[1]
    step = 2.0 * math.pi / FFT
    picked[...] = jnp.transpose(jnp.broadcast_to(index_ref[...], (count, count)))
    channel = jnp.concatenate([picked[pl.ds(i, count // 2, stride=2), :] for i in range(2)], axis=0)
    column = lax.broadcasted_iota(jnp.int32, (count, count), 1)
    fine = ((channel * column) & (FFT - 1)).astype(F32) * step
    coarse = ((channel * (column * LANES)) & (FFT - 1)).astype(F32) * step
    scale = 1.0 / math.sqrt(FFT)
    fine_cos, fine_sin = jnp.cos(fine) * scale, jnp.sin(fine) * scale
    coarse_cos, coarse_sin = jnp.cos(coarse), jnp.sin(coarse)
    for a in range(CHUNKS):
        c, s = coarse_cos[:, a : a + 1], coarse_sin[:, a : a + 1]
        lanes = slice(a * LANES, (a + 1) * LANES)
        table[0:count, lanes] = (c * fine_cos - s * fine_sin).astype(BF16)
        table[count : 2 * count, lanes] = (-(s * fine_cos + c * fine_sin)).astype(BF16)


def correlator_kernel(
    index_ref, order_ref, x_hbm, w_hbm, out_ref,
    x, w, picked, table, filt, dft, stage, send, tail, early, v, p, r1, r2, keep, s3, r3, done,
    load, t_sem, a_send, a_recv, c_send, c_recv, y_send, y_recv, z_send, z_recv,
):
    peers, groups = lax.axis_size("inp"), lax.axis_size("grp")
    channels = p.shape[0]
    me, g = lax.axis_index("inp"), lax.axis_index("grp")
    core, y, z = g % 2, (g // 2) % 4, g // 8
    streams, frames = x.shape[0], x.shape[1] // FFT
    half = frames // 2
    later = (g + 1) % groups

    def y_peer(d):
        return z * 8 + ((y + d) % 4) * 2 + core

    core_peer = g + 1 - 2 * core
    z_peer = (1 - z) * 8 + y * 2 + core
    across = (g + groups - 1 + 2 * core) % groups

    def fetch(number, first, count):
        part = pl.ds(first * FFT, count * FFT)
        return pltpu.make_async_copy(x_hbm.at[:, part], x.at[:, part], load.at[number])

    parts = [
        pltpu.make_async_copy(w_hbm, w, load.at[3]),
        fetch(0, frames - TAPS + 1, TAPS - 1),
        fetch(1, half - TAPS + 1, half),
        fetch(2, 0, half - TAPS + 1),
    ]
    for part in parts:
        part.start()

    barrier = pltpu.get_barrier_semaphore()

    def greet(d, carry):
        pl.semaphore_signal(barrier, inc=1, device_id={"inp": lax.rem(me + d, peers)}, device_id_type=MESH)
        return carry

    lax.fori_loop(1, peers, greet, 0)
    for other in (core_peer, y_peer(1), y_peer(2), y_peer(3), z_peer, across):
        pl.semaphore_signal(barrier, inc=1, device_id={"grp": other}, device_id_type=MESH)

    make_table(index_ref, picked, table)
    parts[0].wait()
    parts[1].wait()

    def filtered(first, count, lo=0, hi=CHUNKS):
        def chunk(at, carry):
            fir(x, w, filt, at, first, count, 0)
            return carry

        lax.fori_loop(lo, hi, chunk, 0)

    filtered(frames, TAPS)
    tail[...] = nt_dot(filt[0 : TAPS * streams, :], table[...]).astype(BF16)
    tail_copy = pltpu.make_async_remote_copy(
        src_ref=tail,
        dst_ref=early,
        send_sem=t_sem.at[0],
        recv_sem=t_sem.at[1],
        device_id={"grp": later},
        device_id_type=MESH,
    )
    parts[2].wait()
    filtered(half, half, 0, CHUNKS // 2)
    pl.semaphore_wait(barrier, peers - 1 + 6)

    @pl.when(g < groups - 1)
    def _():
        tail_copy.start()

    low = lax.broadcasted_iota(jnp.int32, (LANES // 2, LANES), 1) < LANES // 2

    def spectra(h):
        got = nt_dot(filt[...], table[...])
        if h == 0:
            got = jnp.concatenate([got[: TAPS * streams] + early[...].astype(F32), got[TAPS * streams :]], axis=0)
        dft[0] = got[:, :LANES]
        dft[1] = got[:, LANES:]
        for s in range(0, streams, 2):
            rows = [dft[k, pl.ds(s + i, half, stride=streams), :] for i in range(2) for k in range(2)]
            turned = jnp.transpose(jnp.concatenate(rows, axis=0))
            even, odd = turned[: LANES // 2], turned[LANES // 2 :]
            stage[pl.ds(s, LANES // 2, stride=streams), :] = jnp.where(low, even, pltpu.roll(odd, LANES // 2, 1))
            stage[pl.ds(s + 1, LANES // 2, stride=streams), :] = jnp.where(low, pltpu.roll(even, LANES // 2, 1), odd)
        send[h] = stage[...].astype(BF16)

    def turn(h, pair):
        def rows_of(j):
            return pl.ds(pl.multiple_of((j * 2 + pair) * streams, streams), streams)

        here = pl.ds(pl.multiple_of(me * streams, streams), streams)

        def one(d, carry):
            j = lax.rem(me + d, peers)
            pltpu.make_async_remote_copy(
                src_ref=send.at[h, rows_of(j)],
                dst_ref=v.at[h, pair, here],
                send_sem=a_send.at[h, pair],
                recv_sem=a_recv.at[h, pair],
                device_id={"inp": j},
                device_id_type=MESH,
            ).start()
            return carry

        lax.fori_loop(1, peers, one, 0)
        v[h, pair, here] = send[h, rows_of(me)]

    def turn_wait(h, pair, sem):
        part = v.at[h, pair, pl.ds(0, (peers - 1) * streams)]
        pltpu.make_async_copy(part, part, sem.at[h, pair]).wait()

    filtered(half, half, CHUNKS // 2, CHUNKS)
    spectra(1)
    turn(1, 0)
    turn(1, 1)
    parts[3].wait()
    filtered(0, half)

    @pl.when(g > 0)
    def _():
        tail_copy.wait_recv()

    @pl.when(g == 0)
    def _():
        early[...] = jnp.zeros_like(early)

    spectra(0)
    turn(0, 0)
    turn(0, 1)

    def core_copy(c):
        return pltpu.make_async_remote_copy(
            src_ref=p.at[c, 1 - core],
            dst_ref=r1.at[c],
            send_sem=c_send.at[c],
            recv_sem=c_recv.at[c],
            device_id={"grp": core_peer},
            device_id_type=MESH,
        )

    def y_copy(c, d):
        return pltpu.make_async_remote_copy(
            src_ref=p.at[c, core, (y + d) % 4],
            dst_ref=r2.at[c, d - 1],
            send_sem=y_send.at[c, d - 1],
            recv_sem=y_recv.at[c, d - 1],
            device_id={"grp": y_peer(d)},
            device_id_type=MESH,
        )

    def z_copy(c):
        return pltpu.make_async_remote_copy(
            src_ref=s3.at[c],
            dst_ref=r3.at[c],
            send_sem=z_send.at[c],
            recv_sem=z_recv.at[c],
            device_id={"grp": z_peer},
            device_id_type=MESH,
        )

    lanes = lax.broadcasted_iota(jnp.int32, (TILE, LANES), 1)
    quarter = LANES // 4
    scale = 1.0 / math.sqrt(frames * groups)
    order = [zz * 8 + yy * 2 + cc for cc in range(2) for yy in range(4) for zz in range(2)]
    tiles = v.shape[2] // TILE

    def zone(number):
        return jnp.where(lanes // quarter == number, scale, 0.0)

    def products(pair, which):
        c = pair * 2 + which
        keep_re, keep_im = zone(2 * which), zone(2 * which + 1)
        for r in range(tiles):
            left = []
            for h in range(2):
                value = v[h, pair, r * TILE : (r + 1) * TILE].astype(F32)
                plain = (value * (keep_re + keep_im)).reshape(16, 8, LANES)
                cross = pltpu.roll(value, LANES - quarter, 1) * keep_re - pltpu.roll(value, quarter, 1) * keep_im
                cross = cross.reshape(16, 8, LANES)
                left.append(jnp.concatenate([part for o in order for part in (plain[o], cross[o])], axis=0).astype(BF16))
            left = jnp.concatenate(left, axis=1)
            right = jnp.concatenate([v[h, pair, 0 : (r + 1) * TILE] for h in range(2)], axis=1)
            got = nt_dot(left, right).astype(BF16)
            for q in range(r + 1):
                t = r * (r + 1) // 2 + q
                p[c, :, :, :, t * 16 : (t + 1) * 16, :] = got[:, q * TILE : (q + 1) * TILE].reshape(2, 4, 2, 16, LANES)
        core_copy(c).start()

    def core_sum(c):
        core_copy(c).wait_recv()
        for yy in range(4):
            p[c, core, yy] = (p[c, core, yy].astype(F32) + r1[c, yy].astype(F32)).astype(BF16)
        for d in range(1, 4):
            y_copy(c, d).start()

    def y_sum(c):
        for d in range(1, 4):
            y_copy(c, d).wait_recv()
        for zz, mine in ((1 - z, False), (z, True)):
            got = p[c, core, y, zz].astype(F32)
            for d in range(3):
                got = got + r2[c, d, zz].astype(F32)
            if mine:
                keep[c] = got
            else:
                s3[c] = got.astype(BF16)
                z_copy(c).start()

    def gather(pair):
        for h in (1, 0):
            turn_wait(h, pair, a_recv)

    gather(0)
    products(0, 0)
    products(0, 1)
    core_sum(0)
    core_sum(1)
    y_sum(0)
    gather(1)
    products(1, 0)
    products(1, 1)
    core_sum(2)
    y_sum(1)
    core_sum(3)
    y_sum(2)
    y_sum(3)
    for c in range(channels):
        z_copy(c).wait_recv()
        got = keep[c] + r3[c].astype(F32)
        done[c] = got.reshape(done.shape[1:])
        for t in range(done.shape[1]):
            r, q = order_ref[0, t], order_ref[1, t]
            out_ref[c, t] = done[c, r * (r + 1) // 2 + q].reshape(out_ref.shape[2:])

    @pl.when(g < groups - 1)
    def _():
        tail_copy.wait_send()

    for h in range(2):
        for pair in range(2):
            turn_wait(h, pair, a_send)
    for c in range(channels):
        core_copy(c).wait_send()
        for d in range(1, 4):
            y_copy(c, d).wait_send()
        z_copy(c).wait_send()


def shards(samples, channel_index, tile_order):
    streams, length = samples.shape
    frames = length // FFT
    selected = channel_index.shape[0]
    channels = selected // lax.axis_size("inp")
    tile_count = tile_order.shape[0]
    rows = tile_count * 16
    vmem = pl.BlockSpec(memory_space=pltpu.VMEM)
    hbm = pl.BlockSpec(memory_space=pltpu.HBM)
    dma = pltpu.SemaphoreType.DMA
    all_streams = streams * lax.axis_size("inp")
    return pl.pallas_call(
        correlator_kernel,
        out_shape=jax.ShapeDtypeStruct((channels, tile_count, 2, 8, LANES), F32),
        in_specs=[vmem, pl.BlockSpec(memory_space=pltpu.SMEM), hbm, hbm],
        out_specs=vmem,
        scratch_shapes=[
            pltpu.VMEM((streams, length), BF16),
            pltpu.VMEM((TAPS, FFT), F32),
            pltpu.VMEM((selected, selected), jnp.int32),
            pltpu.VMEM((2 * selected, FFT), BF16),
            pltpu.VMEM((streams * frames // 2, FFT), BF16),
            pltpu.VMEM((2, streams * frames // 2, LANES), F32),
            pltpu.VMEM((selected // 2 * streams, LANES), F32),
            pltpu.VMEM((2, selected // 2 * streams, LANES), BF16),
            pltpu.VMEM((TAPS * streams, 2 * selected), BF16),
            pltpu.VMEM((TAPS * streams, 2 * selected), BF16),
            pltpu.VMEM((2, 2, all_streams, LANES), BF16),
            pltpu.VMEM((channels, 2, 4, 2, rows, LANES), BF16),
            pltpu.VMEM((channels, 4, 2, rows, LANES), BF16),
            pltpu.VMEM((channels, 3, 2, rows, LANES), BF16),
            pltpu.VMEM((channels, rows, LANES), F32),
            pltpu.VMEM((channels, rows, LANES), BF16),
            pltpu.VMEM((channels, rows, LANES), BF16),
            pltpu.VMEM((channels, tile_count, 16, LANES), F32),
            dma((4,)),
            dma((2,)),
            dma((2, 2)),
            dma((2, 2)),
            dma((channels,)),
            dma((channels,)),
            dma((channels, 3)),
            dma((channels, 3)),
            dma((channels,)),
            dma((channels,)),
        ],
        compiler_params=pltpu.CompilerParams(collective_id=0, has_side_effects=True, vmem_limit_bytes=61 * 1024 * 1024),
        name="correlator",
    )(channel_index.reshape(1, selected), tile_order.T, samples, jnp.asarray(pfb_window()))


def solution(mesh):
    in_specs = (P("inp", "grp"), P(), P())
    out_specs = P("inp", None, None, "grp", None)
    return jax.shard_map(shards, mesh=mesh, in_specs=in_specs, out_specs=out_specs, check_vma=False)
```

```python
import math

import jax
import jax.numpy as jnp
import numpy as np
from jax import lax
from jax.experimental import pallas as pl
from jax.experimental.pallas import tpu as pltpu
from jax.sharding import PartitionSpec as P

FFT = 2048
TAPS = 16
TILE = 128
LANES = 128
CHUNKS = FFT // LANES
MESH = pl.DeviceIdType.MESH
F32 = jnp.float32
BF16 = jnp.bfloat16


def pfb_window():
    length = TAPS * FFT
    position = np.arange(length, dtype=np.float64)
    offset = (position - length // 2 + 0.5) / FFT
    shaped = np.sinc(offset) * (0.54 - 0.46 * np.cos(2.0 * np.pi * position / (length - 1)))
    shaped = shaped / np.sqrt(np.sum(shaped * shaped) / FFT)
    return shaped.reshape(TAPS, FFT).astype(np.float32)


def nt_dot(a, b):
    return lax.dot_general(a, b, (((1,), (1,)), ((), ())), preferred_element_type=F32)


def is_inner(tap):
    return TAPS // 2 - 2 <= tap < TAPS // 2 + 2


def fir(x_ref, w_ref, filt, at, first, count, row):
    streams, frames = x_ref.shape[0], x_ref.shape[1] // FFT
    lane = pl.multiple_of(at * LANES, LANES)
    taps = []
    for k in range(TAPS):
        weight = w_ref[pl.ds(k, 1), pl.ds(lane, LANES)]
        taps.append(weight if is_inner(k) else jnp.broadcast_to(weight, (streams, LANES)).astype(BF16))
    for start in range(first, first + count, 8):
        inner, outer = [None] * 8, [None] * 8
        for frame in range(max(start - TAPS + 1, 0), min(start + 8, frames)):
            value = x_ref[:, pl.ds(frame * FFT + lane, LANES)]
            wide = value.astype(F32)
            for o in range(8):
                tap = frame - (start + o) + TAPS - 1
                if not 0 <= tap < TAPS:
                    continue
                sums, term = (inner, taps[tap] * wide) if is_inner(tap) else (outer, taps[tap] * value)
                sums[o] = term if sums[o] is None else sums[o] + term
        for o in range(8):
            total = inner[o]
            if outer[o] is not None:
                total = outer[o].astype(F32) if total is None else total + outer[o].astype(F32)
            total = jnp.zeros((streams, LANES), F32) if total is None else total
            to = row + (start - first + o) * streams
            filt[to : to + streams, pl.ds(lane, LANES)] = total.astype(BF16)


def make_table(index_ref, picked, table):
    count = index_ref.shape[1]
    step = 2.0 * math.pi / FFT
    picked[...] = jnp.transpose(jnp.broadcast_to(index_ref[...], (count, count)))
    channel = jnp.concatenate([picked[pl.ds(i, count // 4, stride=4), :] for i in (0, 2, 1, 3)], axis=0)
    column = lax.broadcasted_iota(jnp.int32, (count, count), 1)
    fine = ((channel * column) & (FFT - 1)).astype(F32) * step
    coarse = ((channel * (column * LANES)) & (FFT - 1)).astype(F32) * step
    scale = 1.0 / math.sqrt(FFT)
    fine_cos, fine_sin = jnp.cos(fine) * scale, jnp.sin(fine) * scale
    coarse_cos, coarse_sin = jnp.cos(coarse), jnp.sin(coarse)
    for a in range(CHUNKS):
        c, s = coarse_cos[:, a : a + 1], coarse_sin[:, a : a + 1]
        lanes = slice(a * LANES, (a + 1) * LANES)
        table[0:count, lanes] = (c * fine_cos - s * fine_sin).astype(BF16)
        table[count : 2 * count, lanes] = (-(s * fine_cos + c * fine_sin)).astype(BF16)


def correlator_kernel(
    index_ref, order_ref, x_hbm, w_hbm, out_ref,
    x, w, picked, table, filt, dft, stage, held, send, tail, early, v, p, r1, r2, keep, s3, r3, done,
    load, t_sem, a_send, a_recv, c_send, c_recv, y_send, y_recv, z_send, z_recv,
):
    peers, groups = lax.axis_size("inp"), lax.axis_size("grp")
    units, channels = p.shape[0], out_ref.shape[0]
    me, g = lax.axis_index("inp"), lax.axis_index("grp")
    core, y, z = g % 2, (g // 2) % 4, g // 8
    streams, frames = x.shape[0], x.shape[1] // FFT
    half = frames // 2
    later = (g + 1) % groups

    def y_peer(d):
        return z * 8 + ((y + d) % 4) * 2 + core

    core_peer = g + 1 - 2 * core
    z_peer = (1 - z) * 8 + y * 2 + core
    across = (g + groups - 1 + 2 * core) % groups

    def fetch(number, first, count):
        part = pl.ds(first * FFT, count * FFT)
        return pltpu.make_async_copy(x_hbm.at[:, part], x.at[:, part], load.at[number])

    parts = [
        pltpu.make_async_copy(w_hbm, w, load.at[3]),
        fetch(0, frames - TAPS + 1, TAPS - 1),
        fetch(1, half - TAPS + 1, half),
        fetch(2, 0, half - TAPS + 1),
    ]
    for part in parts:
        part.start()

    barrier = pltpu.get_barrier_semaphore()

    def greet(d, carry):
        pl.semaphore_signal(barrier, inc=1, device_id={"inp": lax.rem(me + d, peers)}, device_id_type=MESH)
        return carry

    lax.fori_loop(1, peers, greet, 0)
    for other in (core_peer, y_peer(1), y_peer(2), y_peer(3), z_peer, across):
        pl.semaphore_signal(barrier, inc=1, device_id={"grp": other}, device_id_type=MESH)

    make_table(index_ref, picked, table)
    parts[0].wait()
    parts[1].wait()

    def filtered(first, count, lo=0, hi=CHUNKS):
        def chunk(at, carry):
            fir(x, w, filt, at, first, count, 0)
            return carry

        lax.fori_loop(lo, hi, chunk, 0)

    filtered(frames, TAPS)
    tail[...] = nt_dot(filt[0 : TAPS * streams, :], table[...]).astype(BF16)
    tail_copy = pltpu.make_async_remote_copy(
        src_ref=tail,
        dst_ref=early,
        send_sem=t_sem.at[0],
        recv_sem=t_sem.at[1],
        device_id={"grp": later},
        device_id_type=MESH,
    )
    parts[2].wait()
    filtered(half, half, 0, CHUNKS // 8)
    pl.semaphore_wait(barrier, peers - 1 + 6)

    @pl.when(g < groups - 1)
    def _():
        tail_copy.start()

    low = lax.broadcasted_iota(jnp.int32, (LANES // 2, LANES), 1) < LANES // 2
    block = peers * streams

    def spectra(h):
        got = nt_dot(filt[...], table[...])
        if h == 0:
            got = jnp.concatenate([got[: TAPS * streams] + early[...].astype(F32), got[TAPS * streams :]], axis=0)
        dft[0] = got[:, :LANES]
        dft[1] = got[:, LANES:]
        for s in range(0, streams, 2):
            rows = [dft[k, pl.ds(s + i, half, stride=streams), :] for i in range(2) for k in range(2)]
            turned = jnp.transpose(jnp.concatenate(rows, axis=0))
            even, odd = turned[: LANES // 2], turned[LANES // 2 :]
            stage[pl.ds(s, LANES // 2, stride=streams), :] = jnp.where(low, even, pltpu.roll(odd, LANES // 2, 1))
            stage[pl.ds(s + 1, LANES // 2, stride=streams), :] = jnp.where(low, pltpu.roll(even, LANES // 2, 1), odd)
        send[1 - h] = stage[:block].astype(BF16)

    def singles():
        first, second = held[...], stage[block:]
        narrow = lax.broadcasted_iota(jnp.int32, first.shape, 1) < LANES // 2
        send[2] = jnp.where(narrow, first, pltpu.roll(second, LANES // 2, 1)).astype(BF16)
        send[3] = jnp.where(narrow, pltpu.roll(first, LANES // 2, 1), second).astype(BF16)

    def turn(b):
        def rows_of(j):
            return pl.ds(pl.multiple_of(j * streams, streams), streams)

        def start(j):
            pltpu.make_async_remote_copy(
                src_ref=send.at[b, rows_of(j)],
                dst_ref=v.at[b, rows_of(me)],
                send_sem=a_send.at[b],
                recv_sem=a_recv.at[b],
                device_id={"inp": j},
                device_id_type=MESH,
            ).start()

        side, deep, wide = me // 16, me // 4 % 4, me % 4

        def across_middle(t, carry):
            start((1 - side) * 16 + (deep + t // 4) % 4 * 4 + (wide + t) % 4)
            return carry

        def same_side(t, carry):
            u = 15 - t
            start(side * 16 + (deep + u // 4) % 4 * 4 + (wide + u) % 4)
            return carry

        lax.fori_loop(0, 16, across_middle, 0)
        lax.fori_loop(0, 15, same_side, 0)
        v[b, rows_of(me)] = send[b, rows_of(me)]

    def turn_wait(b, sem):
        part = v.at[b, pl.ds(0, (peers - 1) * streams)]
        pltpu.make_async_copy(part, part, sem.at[b]).wait()

    filtered(half, half, CHUNKS // 8, CHUNKS)
    spectra(1)
    turn(0)
    held[...] = stage[block:]
    parts[3].wait()
    filtered(0, half)

    @pl.when(g > 0)
    def _():
        tail_copy.wait_recv()

    @pl.when(g == 0)
    def _():
        early[...] = jnp.zeros_like(early)

    spectra(0)
    turn(1)
    singles()

    def core_copy(u):
        return pltpu.make_async_remote_copy(
            src_ref=p.at[u, 1 - core],
            dst_ref=r1.at[u],
            send_sem=c_send.at[u],
            recv_sem=c_recv.at[u],
            device_id={"grp": core_peer},
            device_id_type=MESH,
        )

    def y_copy(u, d):
        return pltpu.make_async_remote_copy(
            src_ref=p.at[u, core, (y + d) % 4],
            dst_ref=r2.at[u, d - 1],
            send_sem=y_send.at[u, d - 1],
            recv_sem=y_recv.at[u, d - 1],
            device_id={"grp": y_peer(d)},
            device_id_type=MESH,
        )

    def z_copy(u):
        return pltpu.make_async_remote_copy(
            src_ref=s3.at[u],
            dst_ref=r3.at[u],
            send_sem=z_send.at[u],
            recv_sem=z_recv.at[u],
            device_id={"grp": z_peer},
            device_id_type=MESH,
        )

    lanes = lax.broadcasted_iota(jnp.int32, (TILE, LANES), 1)
    quarter = LANES // 4
    scale = 1.0 / math.sqrt(frames * groups)
    order = [zz * 8 + yy * 2 + cc for cc in range(2) for yy in range(4) for zz in range(2)]
    tiles = v.shape[1] // TILE
    part = out_ref.shape[1] // 2

    def zone(*numbers):
        return sum(jnp.where(lanes // quarter == number, scale, 0.0) for number in numbers)

    def products(c):
        batches = (0, 1) if c < 2 else (c,)
        re, im = (zone(2 * c), zone(2 * c + 1)) if c < 2 else (zone(0, 2), zone(1, 3))
        for r in range(tiles):
            left = []
            for b in batches:
                value = v[b, r * TILE : (r + 1) * TILE].astype(F32)
                plain = (value * (re + im)).reshape(16, 8, LANES)
                cross = pltpu.roll(value, LANES - quarter, 1) * re - pltpu.roll(value, quarter, 1) * im
                cross = cross.reshape(16, 8, LANES)
                left.append(jnp.concatenate([piece for o in order for piece in (plain[o], cross[o])], axis=0).astype(BF16))
            left = jnp.concatenate(left, axis=1)
            right = jnp.concatenate([v[b, 0 : (r + 1) * TILE] for b in batches], axis=1)
            got = nt_dot(left, right).astype(BF16)
            for q in range(r + 1):
                t = r * (r + 1) // 2 + q
                unit, at = c * 2 + t // part, t % part * 16
                p[unit, :, :, :, at : at + 16, :] = got[:, q * TILE : (q + 1) * TILE].reshape(2, 4, 2, 16, LANES)
            if r == tiles - 2:
                core_copy(c * 2).start()
        core_copy(c * 2 + 1).start()

    def core_sum(u):
        core_copy(u).wait_recv()
        for yy in range(4):
            p[u, core, yy] = (p[u, core, yy].astype(F32) + r1[u, yy].astype(F32)).astype(BF16)
        for d in (2, 1, 3):
            y_copy(u, d).start()

    def y_sum(u):
        for d in range(1, 4):
            y_copy(u, d).wait_recv()
        for zz, mine in ((1 - z, False), (z, True)):
            got = p[u, core, y, zz].astype(F32)
            for d in range(3):
                got = got + r2[u, d, zz].astype(F32)
            if mine:
                keep[u] = got
            else:
                s3[u] = got.astype(BF16)
                z_copy(u).start()

    def z_sum(u):
        z_copy(u).wait_recv()
        done[u // 2, u % 2 * part : (u % 2 + 1) * part] = (keep[u] + r3[u].astype(F32)).reshape((part,) + done.shape[2:])

    turn_wait(1, a_send)
    turn(2)
    turn_wait(0, a_recv)
    turn_wait(1, a_recv)
    products(0)
    products(1)
    turn_wait(2, a_send)
    turn(3)
    for u in (0, 1, 2, 3):
        core_sum(u)
    turn_wait(2, a_recv)
    products(2)
    y_sum(0)
    y_sum(1)
    core_sum(4)
    core_sum(5)
    turn_wait(3, a_recv)
    products(3)
    y_sum(2)
    y_sum(3)
    core_sum(6)
    core_sum(7)
    z_sum(0)
    z_sum(1)
    for u in (4, 5, 6, 7):
        y_sum(u)
    for u in (2, 3, 4, 5, 6, 7):
        z_sum(u)
    for c in range(channels):
        for t in range(done.shape[1]):
            r, q = order_ref[0, t], order_ref[1, t]
            out_ref[c, t] = done[c, r * (r + 1) // 2 + q].reshape(out_ref.shape[2:])

    @pl.when(g < groups - 1)
    def _():
        tail_copy.wait_send()

    turn_wait(0, a_send)
    turn_wait(3, a_send)
    for u in range(units):
        core_copy(u).wait_send()
        for d in range(1, 4):
            y_copy(u, d).wait_send()
        z_copy(u).wait_send()


def shards(samples, channel_index, tile_order):
    streams, length = samples.shape
    frames = length // FFT
    selected = channel_index.shape[0]
    channels = selected // lax.axis_size("inp")
    tile_count = tile_order.shape[0]
    rows = tile_count // 2 * 16
    units = 2 * channels
    vmem = pl.BlockSpec(memory_space=pltpu.VMEM)
    hbm = pl.BlockSpec(memory_space=pltpu.HBM)
    dma = pltpu.SemaphoreType.DMA
    all_streams = streams * lax.axis_size("inp")
    return pl.pallas_call(
        correlator_kernel,
        out_shape=jax.ShapeDtypeStruct((channels, tile_count, 2, 8, LANES), F32),
        in_specs=[vmem, pl.BlockSpec(memory_space=pltpu.SMEM), hbm, hbm],
        out_specs=vmem,
        scratch_shapes=[
            pltpu.VMEM((streams, length), BF16),
            pltpu.VMEM((TAPS, FFT), F32),
            pltpu.VMEM((selected, selected), jnp.int32),
            pltpu.VMEM((2 * selected, FFT), BF16),
            pltpu.VMEM((streams * frames // 2, FFT), BF16),
            pltpu.VMEM((2, streams * frames // 2, LANES), F32),
            pltpu.VMEM((selected // 2 * streams, LANES), F32),
            pltpu.VMEM((all_streams, LANES), F32),
            pltpu.VMEM((4, all_streams, LANES), BF16),
            pltpu.VMEM((TAPS * streams, 2 * selected), BF16),
            pltpu.VMEM((TAPS * streams, 2 * selected), BF16),
            pltpu.VMEM((4, all_streams, LANES), BF16),
            pltpu.VMEM((units, 2, 4, 2, rows, LANES), BF16),
            pltpu.VMEM((units, 4, 2, rows, LANES), BF16),
            pltpu.VMEM((units, 3, 2, rows, LANES), BF16),
            pltpu.VMEM((units, rows, LANES), F32),
            pltpu.VMEM((units, rows, LANES), BF16),
            pltpu.VMEM((units, rows, LANES), BF16),
            pltpu.VMEM((channels, tile_count, 16, LANES), F32),
            dma((4,)),
            dma((2,)),
            dma((4,)),
            dma((4,)),
            dma((units,)),
            dma((units,)),
            dma((units, 3)),
            dma((units, 3)),
            dma((units,)),
            dma((units,)),
        ],
        compiler_params=pltpu.CompilerParams(collective_id=0, has_side_effects=True, vmem_limit_bytes=61 * 1024 * 1024),
        name="correlator",
    )(channel_index.reshape(1, selected), tile_order.T, samples, jnp.asarray(pfb_window()))


def solution(mesh):
    in_specs = (P("inp", "grp"), P(), P())
    out_specs = P("inp", None, None, "grp", None)
    return jax.shard_map(shards, mesh=mesh, in_specs=in_specs, out_specs=out_specs, check_vma=False)
```

```python
import math

import jax
import jax.numpy as jnp
import numpy as np
from jax import lax
from jax.experimental import pallas as pl
from jax.experimental.pallas import tpu as pltpu
from jax.sharding import PartitionSpec as P

FFT = 2048
TAPS = 16
TILE = 128
LANES = 128
CHUNKS = FFT // LANES
MESH = pl.DeviceIdType.MESH
F32 = jnp.float32
BF16 = jnp.bfloat16


def pfb_window():
    length = TAPS * FFT
    position = np.arange(length, dtype=np.float64)
    offset = (position - length // 2 + 0.5) / FFT
    shaped = np.sinc(offset) * (0.54 - 0.46 * np.cos(2.0 * np.pi * position / (length - 1)))
    shaped = shaped / np.sqrt(np.sum(shaped * shaped) / FFT)
    return shaped.reshape(TAPS, FFT).astype(np.float32)


def nt_dot(a, b):
    return lax.dot_general(a, b, (((1,), (1,)), ((), ())), preferred_element_type=F32)


def is_inner(tap):
    return TAPS // 2 - 1 <= tap < TAPS // 2 + 1


def fir(x_ref, w_ref, filt, at, first, count, row):
    streams, frames = x_ref.shape[0], x_ref.shape[1] // FFT
    lane = pl.multiple_of(at * LANES, LANES)
    taps = []
    for k in range(TAPS):
        weight = w_ref[pl.ds(k, 1), pl.ds(lane, LANES)]
        taps.append(weight if is_inner(k) else jnp.broadcast_to(weight, (streams, LANES)).astype(BF16))
    for start in range(first, first + count, 8):
        inner, outer = [None] * 8, [None] * 8
        for frame in range(max(start - TAPS + 1, 0), min(start + 8, frames)):
            value = x_ref[:, pl.ds(frame * FFT + lane, LANES)]
            wide = value.astype(F32)
            for o in range(8):
                tap = frame - (start + o) + TAPS - 1
                if not 0 <= tap < TAPS:
                    continue
                sums, term = (inner, taps[tap] * wide) if is_inner(tap) else (outer, taps[tap] * value)
                sums[o] = term if sums[o] is None else sums[o] + term
        for o in range(8):
            total = inner[o]
            if outer[o] is not None:
                total = outer[o].astype(F32) if total is None else total + outer[o].astype(F32)
            total = jnp.zeros((streams, LANES), F32) if total is None else total
            to = row + (start - first + o) * streams
            filt[to : to + streams, pl.ds(lane, LANES)] = total.astype(BF16)


def make_table(index_ref, picked, table):
    count = index_ref.shape[1]
    step = 2.0 * math.pi / FFT
    picked[...] = jnp.transpose(jnp.broadcast_to(index_ref[...], (count, count)))
    channel = jnp.concatenate([picked[pl.ds(i, count // 4, stride=4), :] for i in (0, 2, 1, 3)], axis=0)
    column = lax.broadcasted_iota(jnp.int32, (count, count), 1)
    fine = ((channel * column) & (FFT - 1)).astype(F32) * step
    coarse = ((channel * (column * LANES)) & (FFT - 1)).astype(F32) * step
    scale = 1.0 / math.sqrt(FFT)
    fine_cos, fine_sin = jnp.cos(fine) * scale, jnp.sin(fine) * scale
    coarse_cos, coarse_sin = jnp.cos(coarse), jnp.sin(coarse)
    for a in range(CHUNKS):
        c, s = coarse_cos[:, a : a + 1], coarse_sin[:, a : a + 1]
        lanes = slice(a * LANES, (a + 1) * LANES)
        table[0:count, lanes] = (c * fine_cos - s * fine_sin).astype(BF16)
        table[count : 2 * count, lanes] = (-(s * fine_cos + c * fine_sin)).astype(BF16)


def correlator_kernel(
    index_ref, order_ref, x_hbm, w_hbm, out_ref,
    x, w, picked, table, filt, dft, stage, held, send, tail, early, v, p, r1, r2, keep, s3, r3, done,
    load, t_sem, a_send, a_recv, c_send, c_recv, y_send, y_recv, z_send, z_recv,
):
    peers, groups = lax.axis_size("inp"), lax.axis_size("grp")
    units, channels = p.shape[0], out_ref.shape[0]
    me, g = lax.axis_index("inp"), lax.axis_index("grp")
    core, y, z = g % 2, (g // 2) % 4, g // 8
    streams, frames = x.shape[0], x.shape[1] // FFT
    half = frames // 2
    later = (g + 1) % groups

    def y_peer(d):
        return z * 8 + ((y + d) % 4) * 2 + core

    core_peer = g + 1 - 2 * core
    z_peer = (1 - z) * 8 + y * 2 + core
    across = (g + groups - 1 + 2 * core) % groups

    def fetch(number, first, count):
        part = pl.ds(first * FFT, count * FFT)
        return pltpu.make_async_copy(x_hbm.at[:, part], x.at[:, part], load.at[number])

    parts = [
        pltpu.make_async_copy(w_hbm, w, load.at[3]),
        fetch(0, frames - TAPS + 1, TAPS - 1),
        fetch(1, half - TAPS + 1, half),
        fetch(2, 0, half - TAPS + 1),
    ]
    for part in parts:
        part.start()

    barrier = pltpu.get_barrier_semaphore()

    def greet(d, carry):
        pl.semaphore_signal(barrier, inc=1, device_id={"inp": lax.rem(me + d, peers)}, device_id_type=MESH)
        return carry

    lax.fori_loop(1, peers, greet, 0)
    for other in (core_peer, y_peer(1), y_peer(2), y_peer(3), z_peer, across):
        pl.semaphore_signal(barrier, inc=1, device_id={"grp": other}, device_id_type=MESH)

    make_table(index_ref, picked, table)
    parts[0].wait()
    parts[1].wait()

    def filtered(first, count, lo=0, hi=CHUNKS):
        def chunk(at, carry):
            fir(x, w, filt, at, first, count, 0)
            return carry

        lax.fori_loop(lo, hi, chunk, 0)

    filtered(frames, TAPS)
    tail[...] = nt_dot(filt[0 : TAPS * streams, :], table[...]).astype(BF16)
    tail_copy = pltpu.make_async_remote_copy(
        src_ref=tail,
        dst_ref=early,
        send_sem=t_sem.at[0],
        recv_sem=t_sem.at[1],
        device_id={"grp": later},
        device_id_type=MESH,
    )
    parts[2].wait()
    filtered(half, half, 0, CHUNKS // 8)
    pl.semaphore_wait(barrier, peers - 1 + 6)

    @pl.when(g < groups - 1)
    def _():
        tail_copy.start()

    low = lax.broadcasted_iota(jnp.int32, (LANES // 2, LANES), 1) < LANES // 2
    block = peers * streams

    def spectra(h):
        got = nt_dot(filt[...], table[...])
        if h == 0:
            got = jnp.concatenate([got[: TAPS * streams] + early[...].astype(F32), got[TAPS * streams :]], axis=0)
        dft[0] = got[:, :LANES]
        dft[1] = got[:, LANES:]
        for s in range(0, streams, 2):
            rows = [dft[k, pl.ds(s + i, half, stride=streams), :] for i in range(2) for k in range(2)]
            turned = jnp.transpose(jnp.concatenate(rows, axis=0))
            even, odd = turned[: LANES // 2], turned[LANES // 2 :]
            stage[pl.ds(s, LANES // 2, stride=streams), :] = jnp.where(low, even, pltpu.roll(odd, LANES // 2, 1))
            stage[pl.ds(s + 1, LANES // 2, stride=streams), :] = jnp.where(low, pltpu.roll(even, LANES // 2, 1), odd)
        send[1 - h] = stage[:block].astype(BF16)

    def singles():
        first, second = held[...], stage[block:]
        narrow = lax.broadcasted_iota(jnp.int32, first.shape, 1) < LANES // 2
        send[2] = jnp.where(narrow, first, pltpu.roll(second, LANES // 2, 1)).astype(BF16)
        send[3] = jnp.where(narrow, pltpu.roll(first, LANES // 2, 1), second).astype(BF16)

    def turn(b):
        def rows_of(j):
            return pl.ds(pl.multiple_of(j * streams, streams), streams)

        def start(j):
            pltpu.make_async_remote_copy(
                src_ref=send.at[b, rows_of(j)],
                dst_ref=v.at[b, rows_of(me)],
                send_sem=a_send.at[b],
                recv_sem=a_recv.at[b],
                device_id={"inp": j},
                device_id_type=MESH,
            ).start()

        side, deep, wide = me // 16, me // 4 % 4, me % 4

        def across_middle(t, carry):
            start((1 - side) * 16 + (deep + t // 4) % 4 * 4 + (wide + t) % 4)
            return carry

        def same_side(t, carry):
            u = 15 - t
            start(side * 16 + (deep + u // 4) % 4 * 4 + (wide + u) % 4)
            return carry

        lax.fori_loop(0, 16, across_middle, 0)
        lax.fori_loop(0, 15, same_side, 0)
        v[b, rows_of(me)] = send[b, rows_of(me)]

    def turn_wait(b, sem):
        part = v.at[b, pl.ds(0, (peers - 1) * streams)]
        pltpu.make_async_copy(part, part, sem.at[b]).wait()

    filtered(half, half, CHUNKS // 8, CHUNKS)
    spectra(1)
    turn(0)
    held[...] = stage[block:]
    parts[3].wait()
    filtered(0, half)

    @pl.when(g > 0)
    def _():
        tail_copy.wait_recv()

    @pl.when(g == 0)
    def _():
        early[...] = jnp.zeros_like(early)

    spectra(0)
    turn(1)
    singles()

    def core_copy(u):
        return pltpu.make_async_remote_copy(
            src_ref=p.at[u, 1 - core],
            dst_ref=r1.at[u],
            send_sem=c_send.at[u],
            recv_sem=c_recv.at[u],
            device_id={"grp": core_peer},
            device_id_type=MESH,
        )

    def y_copy(u, d):
        return pltpu.make_async_remote_copy(
            src_ref=p.at[u, core, (y + d) % 4],
            dst_ref=r2.at[u, d - 1],
            send_sem=y_send.at[u, d - 1],
            recv_sem=y_recv.at[u, d - 1],
            device_id={"grp": y_peer(d)},
            device_id_type=MESH,
        )

    def z_copy(u):
        return pltpu.make_async_remote_copy(
            src_ref=s3.at[u],
            dst_ref=r3.at[u],
            send_sem=z_send.at[u],
            recv_sem=z_recv.at[u],
            device_id={"grp": z_peer},
            device_id_type=MESH,
        )

    lanes = lax.broadcasted_iota(jnp.int32, (TILE, LANES), 1)
    quarter = LANES // 4
    scale = 1.0 / math.sqrt(frames * groups)
    order = [zz * 8 + yy * 2 + cc for cc in range(2) for yy in range(4) for zz in range(2)]
    tiles = v.shape[1] // TILE
    part = out_ref.shape[1] // 2

    def zone(*numbers):
        return sum(jnp.where(lanes // quarter == number, scale, 0.0) for number in numbers)

    def products(c):
        batches = (0, 1) if c < 2 else (c,)
        re, im = (zone(2 * c), zone(2 * c + 1)) if c < 2 else (zone(0, 2), zone(1, 3))
        for r in range(tiles):
            left = []
            for b in batches:
                value = v[b, r * TILE : (r + 1) * TILE].astype(F32)
                plain = (value * (re + im)).reshape(16, 8, LANES)
                cross = pltpu.roll(value, LANES - quarter, 1) * re - pltpu.roll(value, quarter, 1) * im
                cross = cross.reshape(16, 8, LANES)
                left.append(jnp.concatenate([piece for o in order for piece in (plain[o], cross[o])], axis=0).astype(BF16))
            left = jnp.concatenate(left, axis=1)
            right = jnp.concatenate([v[b, 0 : (r + 1) * TILE] for b in batches], axis=1)
            got = nt_dot(left, right).astype(BF16)
            for q in range(r + 1):
                t = r * (r + 1) // 2 + q
                unit, at = c * 2 + t // part, t % part * 16
                p[unit, :, :, :, at : at + 16, :] = got[:, q * TILE : (q + 1) * TILE].reshape(2, 4, 2, 16, LANES)
            if r == tiles - 2:
                core_copy(c * 2).start()
        core_copy(c * 2 + 1).start()

    def core_sum(u):
        core_copy(u).wait_recv()
        for yy in range(4):
            p[u, core, yy] = (p[u, core, yy].astype(F32) + r1[u, yy].astype(F32)).astype(BF16)
        for d in (2, 1, 3):
            y_copy(u, d).start()

    def y_sum(u):
        for d in range(1, 4):
            y_copy(u, d).wait_recv()
        for zz, mine in ((1 - z, False), (z, True)):
            got = p[u, core, y, zz].astype(F32)
            for d in range(3):
                got = got + r2[u, d, zz].astype(F32)
            if mine:
                keep[u] = got
            else:
                s3[u] = got.astype(BF16)
                z_copy(u).start()

    def z_sum(u):
        z_copy(u).wait_recv()
        done[u // 2, u % 2 * part : (u % 2 + 1) * part] = (keep[u] + r3[u].astype(F32)).reshape((part,) + done.shape[2:])

    def y_left(u):
        for d in range(1, 4):
            y_copy(u, d).wait_send()

    turn_wait(1, a_send)
    turn(2)
    turn_wait(0, a_recv)
    turn_wait(1, a_recv)
    products(0)
    products(1)
    core_sum(0)
    core_sum(1)
    turn_wait(2, a_send)
    turn(3)
    turn_wait(2, a_recv)
    products(2)
    y_left(0)
    y_left(1)
    core_sum(2)
    core_sum(3)
    y_sum(0)
    y_sum(1)
    y_left(2)
    y_left(3)
    core_sum(4)
    core_sum(5)
    turn_wait(3, a_recv)
    products(3)
    y_sum(2)
    y_sum(3)
    y_left(4)
    y_left(5)
    core_sum(6)
    core_sum(7)
    y_sum(4)
    y_sum(5)
    y_sum(6)
    y_sum(7)
    z_sum(0)
    z_sum(1)
    z_sum(2)
    z_sum(3)
    z_sum(4)
    z_sum(5)
    z_sum(6)
    z_sum(7)
    for c in range(channels):
        for t in range(done.shape[1]):
            r, q = order_ref[0, t], order_ref[1, t]
            out_ref[c, t] = done[c, r * (r + 1) // 2 + q].reshape(out_ref.shape[2:])

    @pl.when(g < groups - 1)
    def _():
        tail_copy.wait_send()

    turn_wait(0, a_send)
    turn_wait(3, a_send)
    for u in range(units):
        core_copy(u).wait_send()
        if u >= 6:
            y_left(u)
        z_copy(u).wait_send()


def shards(samples, channel_index, tile_order):
    streams, length = samples.shape
    frames = length // FFT
    selected = channel_index.shape[0]
    channels = selected // lax.axis_size("inp")
    tile_count = tile_order.shape[0]
    rows = tile_count // 2 * 16
    units = 2 * channels
    vmem = pl.BlockSpec(memory_space=pltpu.VMEM)
    hbm = pl.BlockSpec(memory_space=pltpu.HBM)
    dma = pltpu.SemaphoreType.DMA
    all_streams = streams * lax.axis_size("inp")
    return pl.pallas_call(
        correlator_kernel,
        out_shape=jax.ShapeDtypeStruct((channels, tile_count, 2, 8, LANES), F32),
        in_specs=[vmem, pl.BlockSpec(memory_space=pltpu.SMEM), hbm, hbm],
        out_specs=vmem,
        scratch_shapes=[
            pltpu.VMEM((streams, length), BF16),
            pltpu.VMEM((TAPS, FFT), F32),
            pltpu.VMEM((selected, selected), jnp.int32),
            pltpu.VMEM((2 * selected, FFT), BF16),
            pltpu.VMEM((streams * frames // 2, FFT), BF16),
            pltpu.VMEM((2, streams * frames // 2, LANES), F32),
            pltpu.VMEM((selected // 2 * streams, LANES), F32),
            pltpu.VMEM((all_streams, LANES), F32),
            pltpu.VMEM((4, all_streams, LANES), BF16),
            pltpu.VMEM((TAPS * streams, 2 * selected), BF16),
            pltpu.VMEM((TAPS * streams, 2 * selected), BF16),
            pltpu.VMEM((4, all_streams, LANES), BF16),
            pltpu.VMEM((units, 2, 4, 2, rows, LANES), BF16),
            pltpu.VMEM((units, 4, 2, rows, LANES), BF16),
            pltpu.VMEM((units, 3, 2, rows, LANES), BF16),
            pltpu.VMEM((units, rows, LANES), F32),
            pltpu.VMEM((units, rows, LANES), BF16),
            pltpu.VMEM((units, rows, LANES), BF16),
            pltpu.VMEM((channels, tile_count, 16, LANES), F32),
            dma((4,)),
            dma((2,)),
            dma((4,)),
            dma((4,)),
            dma((units,)),
            dma((units,)),
            dma((units, 3)),
            dma((units, 3)),
            dma((units,)),
            dma((units,)),
        ],
        compiler_params=pltpu.CompilerParams(collective_id=0, has_side_effects=True, vmem_limit_bytes=61 * 1024 * 1024),
        name="correlator",
    )(channel_index.reshape(1, selected), tile_order.T, samples, jnp.asarray(pfb_window()))


def solution(mesh):
    in_specs = (P("inp", "grp"), P(), P())
    out_specs = P("inp", None, None, "grp", None)
    return jax.shard_map(shards, mesh=mesh, in_specs=in_specs, out_specs=out_specs, check_vma=False)
```
